256 devices in a mesh: days: 8 (over z), row: 2 (over core), col: 16 (over x, y).
Axes of the slice: x: 4, y: 4, z: 8, core: 2. Of those that a mesh axis runs over, the one named last changes fastest.
Arguments:
- inverse_blocks: bfloat16 [16, 1024, 1024], P('days', 'col', 'row'), may hold values from -1 to 1, as said below
- factor_blocks: bfloat16 [16, 1024, 1024], P('days', 'col', 'row'), may hold values from -1.1 to 1.1
- sigma_end: bfloat16 [1024, 1024], P('col', 'row'), may hold values from -5 to 5, as said below
Outputs:
- marginal_covariance: bfloat16 [16, 1024, 1024], P('days', 'col', 'row')
- cross_covariance: bfloat16 [16, 1024, 1024], P('days', 'col', 'row')
The draws below stay inside these ranges and needn't reach their ends.
Inputs may be any that keep to these rules, and one draw needn't show every extreme that they name: `inverse_blocks`: each day's block is symmetric. `sigma_end`: symmetric.
All inputs are finite; a program needn't handle non-finite values.
Results may differ from the reference program's by a relative error of at most 0.0025.
The reference program's roundings to bfloat16 on the way count: a program that leaves them out, or rounds other values in their place, can miss the bound.
Values may be sent and summed in bfloat16 or wider, within the bound.
No kernel may reach another device: no remote copies, remote signals or barrier semaphores. Data moves between devices by JAX's collectives and lax.ppermute only.
A program may use at most 64 MiB of HBM per device.

```python
import math
import jax
import jax.numpy as jnp
from jax import lax

NODES = 1024
DAYS_DEV = 2
HORIZON_LENGTH = 16
N_DAYS = 8


def symmetric_blocks(noise, key_diag, lowest, highest, spread):
    diagonal = jnp.exp(jax.random.uniform(key_diag, noise.shape[:-1], jnp.float32, math.log(lowest), math.log(highest)))
    identity = jnp.eye(noise.shape[-1], dtype=jnp.float32)
    mixed = (noise + jnp.swapaxes(noise, -1, -2)) * (spread / math.sqrt(noise.shape[-1]))
    return mixed + identity * diagonal[..., None, :]


def draw_inverse_blocks(key, part):
    key = jax.random.fold_in(key, 11)
    perturbation_seed, key_diag = jax.random.split(key)
    noise = jnp.clip(jax.random.normal(perturbation_seed, (HORIZON_LENGTH, NODES, NODES), jnp.float32), -4.0, 4.0)
    return symmetric_blocks(noise, key_diag, 0.1, 0.4, 0.06).astype(jnp.bfloat16)


def draw_sigma_end(key, part):
    key = jax.random.fold_in(key, 37)
    perturbation_seed, key_diag = jax.random.split(key)
    noise = jnp.clip(jax.random.normal(perturbation_seed, (NODES, NODES), jnp.float32), -4.0, 4.0)
    return symmetric_blocks(noise, key_diag, 1.0, 4.0, 0.3).astype(jnp.bfloat16)


def draw_factor_blocks(key, part):
    key = jax.random.fold_in(key, 23)
    perturbation_seed, picking_random_seed, smooth_random_seed, rapid_random_seed, spike_random_seed = jax.random.split(key, 5)
    noise = jnp.clip(jax.random.normal(perturbation_seed, (HORIZON_LENGTH, NODES, NODES), jnp.float32), -4.0, 4.0)
    slow_share = 0.5
    chooser = jax.random.uniform(picking_random_seed, (NODES,), jnp.float32) < slow_share
    slow_rate = jax.random.uniform(smooth_random_seed, (NODES,), jnp.float32, 0.93, 0.99)
    fast_rate = jax.random.uniform(rapid_random_seed, (NODES,), jnp.float32, 0.3, 0.6)
    autocorrelation_factor = jnp.where(chooser, slow_rate, fast_rate)
    spike_occurrences = jnp.where(jax.random.uniform(spike_random_seed, (HORIZON_LENGTH, 1), jnp.float32) < 0.15, 0.6, 1.0)
    identity = jnp.eye(NODES, dtype=jnp.float32)
    decay_coefficient = autocorrelation_factor[None, :] * spike_occurrences
    return (noise * (0.2 / math.sqrt(NODES)) + identity * decay_coefficient[:, None, :]).astype(jnp.bfloat16)


def setup_inputs(seed: int = 0) -> dict:
    streams_of = jax.random.split(jax.random.key(seed), 4)
    return {
        "inverse_blocks": draw_inverse_blocks(jax.random.fold_in(streams_of[3], 71), 0),
        "factor_blocks": draw_factor_blocks(jax.random.fold_in(streams_of[3], 71), 0),
        "sigma_end": draw_sigma_end(jax.random.fold_in(streams_of[3], 71), 0),
    }


def reference(inverse_blocks, factor_blocks, sigma_end):
    separator = sigma_end.astype(jnp.float32)
    marginal = [None] * (DAYS_DEV * N_DAYS)
    crossing = [None] * (DAYS_DEV * N_DAYS)
    for block_index in range(N_DAYS - 1, -1, -1):
        following = separator.astype(jnp.bfloat16)
        for within in range(DAYS_DEV - 1, -1, -1):
            day_index = block_index * DAYS_DEV + within
            factor = factor_blocks[day_index]
            product = jnp.dot(following, factor, preferred_element_type=jnp.float32).astype(jnp.bfloat16)
            updated = inverse_blocks[day_index].astype(jnp.float32) + jnp.dot(factor.T, product, preferred_element_type=jnp.float32)
            following = updated.astype(jnp.bfloat16)
            marginal[day_index] = following
            crossing[day_index] = product
        for within in range(DAYS_DEV - 1, -1, -1):
            day_index = block_index * DAYS_DEV + within
            factor_wide = factor_blocks[day_index].astype(jnp.float32)
            inner_product = jnp.dot(separator, factor_wide, preferred_element_type=jnp.float32, precision=lax.Precision.HIGHEST)
            separator = inverse_blocks[day_index].astype(jnp.float32) + jnp.dot(factor_wide.T, inner_product, preferred_element_type=jnp.float32, precision=lax.Precision.HIGHEST)
    return jnp.stack(marginal), jnp.stack(crossing)
```

```python
import jax
import jax.numpy as jnp
from jax import lax
from jax.sharding import PartitionSpec as P

narrow = jnp.bfloat16
wide = jnp.float32


def shifted(value, steps):
    count = lax.axis_size("days")
    return lax.ppermute(value, "days", [(source, source - steps) for source in range(steps, count)])


def other_core(value):
    return lax.ppermute(value, "row", [(0, 1), (1, 0)])


def ordered(own, other, axis):
    first = lax.axis_index("row") == 0
    return jnp.concatenate([jnp.where(first, own, other), jnp.where(first, other, own)], axis=axis)


def both_cores(value, axis):
    return ordered(value, other_core(value), axis)


def spread(value):
    count = lax.axis_size("col")
    return lax.all_to_all(
        jnp.broadcast_to(value[None], (count,) + value.shape), "col", 0, 0, tiled=True
    )


def halves(value):
    high = lax.reduce_precision(value, 8, 7)
    return (high.astype(narrow), (value - high).astype(narrow))


def product(left, right):
    return jnp.dot(left, right, preferred_element_type=wide)


def product_t(left, right):
    return lax.dot_general(left, right, (((0,), (0,)), ((), ())), preferred_element_type=wide)


def rows_times(rows, factor_parts):
    count, width = rows.shape[0], factor_parts.shape[1] // 2
    split = product(jnp.concatenate(halves(rows), 0), factor_parts)
    return (
        split[:count, :width]
        + split[:count, width:]
        + split[count:, :width]
        + split[count:, width:]
    )


def cols_times(cols, factor_parts):
    count, width = cols.shape[1], factor_parts.shape[1] // 2
    split = product_t(jnp.concatenate(halves(cols), 1), factor_parts)
    return (
        split[:count, :width]
        + split[:count, width:]
        + split[count:, :width]
        + split[count:, width:]
    )


def turned(rows):
    chips = lax.axis_size("col")
    count, width = rows.shape
    blocks = rows.reshape(count, chips, width // chips).transpose(1, 0, 2)
    return lax.all_to_all(blocks, "col", 0, 0, tiled=True).reshape(chips * count, width // chips)


def shards(inverse_blocks, factor_blocks, sigma_end):
    chips = lax.axis_size("col")
    days, rows, half = factor_blocks.shape
    nodes = chips * rows
    strip = rows // 2
    core = lax.axis_index("row")
    chip = lax.axis_index("col")
    group = lax.axis_index("days")
    final_group = group == lax.axis_size("days") - 1

    inverse_last = lax.all_gather(inverse_blocks[1], "col", axis=0, tiled=True)

    mine = spread(factor_blocks.reshape(days * rows, half)).reshape(chips, days, rows, half)
    theirs = other_core(mine)
    full = ordered(mine, theirs, 3)
    factor_first = full[:, 0].reshape(nodes, nodes)
    factor_last = full[:, 1].reshape(nodes, nodes)

    node = lax.broadcasted_iota(jnp.int32, (nodes, half), 0)
    slot = lax.broadcasted_iota(jnp.int32, (nodes, half), 1)
    chosen = node == (slot // strip) * rows + core * strip + slot % strip
    factor_first_core = product(factor_first, chosen.astype(narrow)).astype(narrow)
    transfer = jnp.concatenate(halves(product(factor_last, factor_first)), 1)
    transfer_core = jnp.concatenate(halves(product(factor_last, factor_first_core)), 1)

    fixed = both_cores(
        jnp.stack([inverse_blocks[0], inverse_blocks[1], sigma_end]), 2
    )
    inverse_first_rows, inverse_last_rows, sigma_rows = (fixed[0], fixed[1], fixed[2])
    strip_start = core * strip
    inverse_first_strip = lax.dynamic_slice_in_dim(inverse_first_rows, strip_start, strip, 0)
    sigma_strip = lax.dynamic_slice_in_dim(sigma_rows, strip_start, strip, 0)

    from_inverse = product(inverse_last_rows, factor_first_core)
    started = jnp.where(final_group, sigma_rows, jnp.zeros_like(sigma_rows))
    from_sigma = product(started, transfer_core)
    from_sigma = from_sigma[:, :half] + from_sigma[:, half:]
    pair = turned(jnp.concatenate([from_inverse, from_sigma], 0)).reshape(chips, 2, rows, strip)
    inverse_part = pair[:, 0].reshape(nodes, strip)
    sigma_part = pair[:, 1].reshape(nodes, strip)
    inverse_term = product_t(jnp.concatenate(halves(inverse_part), 1), factor_first)
    first_map = (
        inverse_first_strip.astype(wide)
        + inverse_term[:strip]
        + inverse_term[strip:]
        + cols_times(sigma_part, transfer)
    )
    state = first_map
    for _ in range(lax.axis_size("days") - 2):
        arrived = both_cores(shifted(state, 1), 0)
        state = first_map + cols_times(turned(rows_times(arrived, transfer_core)), transfer)

    separator = jnp.where(final_group, sigma_strip, shifted(state, 1).astype(narrow))
    strips = spread(separator)
    covariance = ordered(strips, other_core(strips), 1).reshape(nodes, nodes)

    inverse_last_full = both_cores(inverse_last, 1)
    cross_last = product(covariance, factor_last).astype(narrow)
    marginal_last = (
        inverse_last_full.astype(wide) + product_t(factor_last, cross_last)
    ).astype(narrow)
    factor_first_half = mine[:, 0].reshape(nodes, half)
    cross_first_half = product(marginal_last, factor_first_half).astype(narrow)
    factor_first_rows = lax.dynamic_slice_in_dim(factor_first, chip * rows, rows, 1)
    marginal_first = (
        inverse_blocks[0].astype(wide) + product_t(factor_first_rows, cross_first_half)
    ).astype(narrow)

    def own(value):
        return lax.dynamic_slice(value, (chip * rows, core * half), (rows, half))

    cross_first = lax.dynamic_slice_in_dim(cross_first_half, chip * rows, rows, 0)
    return (
        jnp.stack([marginal_first, own(marginal_last)]),
        jnp.stack([cross_first, own(cross_last)]),
    )


def solution(mesh):
    placed = (P("days", "col", "row"), P("days", "col", "row"), P("col", "row"))
    return jax.shard_map(
        shards,
        mesh=mesh,
        in_specs=placed,
        out_specs=(P("days", "col", "row"), P("days", "col", "row")),
        check_vma=False,
    )
```

```python
import jax
import jax.numpy as jnp
from jax import lax
from jax.experimental import pallas as pl
from jax.experimental.pallas import tpu as pltpu
from jax.sharding import PartitionSpec as P

narrow = jnp.bfloat16
wide = jnp.float32
STRIP = 32
PACK = 8
VMEM_LIMIT = 20 * 1024 * 1024


def shifted(value, steps, sources=None):
    count = lax.axis_size("days")
    sources = range(steps, count) if sources is None else sources
    return lax.ppermute(value, "days", [(source, source - steps) for source in sources])


def other_core(value):
    return lax.ppermute(value, "row", [(0, 1), (1, 0)])


def ordered(own, other, axis):
    first = lax.axis_index("row") == 0
    return jnp.concatenate([jnp.where(first, own, other), jnp.where(first, other, own)], axis=axis)


def both_cores(value, axis):
    return ordered(value, other_core(value), axis)


def spread(value):
    count = lax.axis_size("col")
    return lax.all_to_all(
        jnp.broadcast_to(value[None], (count,) + value.shape), "col", 0, 0, tiled=True
    )


def halves(value):
    high = value.astype(narrow)
    return (high, (value - high.astype(wide)).astype(narrow))


def times(pieces, factor_ref, day):
    _, chips, rows, nodes = factor_ref.shape
    return jnp.dot(
        pieces, factor_ref[day].reshape(chips * rows, nodes), preferred_element_type=wide
    )


def times_wide(rows, factor_ref, day):
    split = times(jnp.concatenate(halves(rows), 0), factor_ref, day)
    count = rows.shape[0]
    return split[:count] + split[count:]


def pack(rows, out_ref, place):
    devices = out_ref.shape[0]
    chips = devices // 2
    padded = jnp.concatenate([rows, jnp.zeros((128 - STRIP, rows.shape[1]), wide)], axis=0)
    turned = padded.T
    for core in range(2):
        for chip in range(chips):
            start = (2 * chip + core) * STRIP
            for part in range(STRIP // PACK):
                out_ref[
                    core * chips + chip,
                    place * PACK : (place + 1) * PACK,
                    part * STRIP : (part + 1) * STRIP,
                ] = turned[start + part * PACK : start + (part + 1) * PACK, :STRIP]


def unpack(in_ref, place, rows_ref):
    devices = in_ref.shape[0]
    chips = devices // 2
    for core in range(2):
        for chip in range(chips):
            start = (2 * chip + core) * STRIP
            for part in range(STRIP // PACK):
                rows_ref[part * PACK : (part + 1) * PACK, start : start + STRIP] = in_ref[
                    core * chips + chip,
                    place * PACK : (place + 1) * PACK,
                    part * STRIP : (part + 1) * STRIP,
                ]


def stage(own_ref, other_ref, out_ref, sems):
    core = lax.axis_index("row")
    days, _, _, nodes = out_ref.shape
    half = nodes // 2
    copies = []
    for day in range(days):
        for which, (ref, place) in enumerate(((own_ref, core), (other_ref, 1 - core))):
            start = pl.multiple_of(place * half, half)
            copies.append(
                pltpu.make_async_copy(
                    ref.at[:, day],
                    out_ref.at[day, :, :, pl.ds(start, half)],
                    sems.at[2 * day + which],
                )
            )
    for copy in copies:
        copy.start()
    for copy in copies:
        copy.wait()


def staged(own, other):
    chips, days, rows, half = own.shape
    return pl.pallas_call(
        stage,
        out_shape=pltpu.VMEM((days, chips, rows, 2 * half), narrow),
        in_specs=[pl.BlockSpec(memory_space=pl.ANY)] * 2,
        out_specs=pl.BlockSpec(memory_space=pltpu.VMEM),
        scratch_shapes=[pltpu.SemaphoreType.DMA((2 * days,))],
        compiler_params=pltpu.CompilerParams(vmem_limit_bytes=VMEM_LIMIT),
    )(own, other)


def first_out(inverse_ref, sigma_ref, factor_ref, out_ref):
    later = times(sigma_ref[...], factor_ref, 1)
    stacked = jnp.concatenate([inverse_ref[...], *halves(later)], 0)
    split = times(stacked, factor_ref, 0)
    pack(split[:STRIP], out_ref, 0)
    pack(split[STRIP : 2 * STRIP] + split[2 * STRIP :], out_ref, 1)


def first_in(packed_ref, base_ref, factor_ref, out_ref, near_ref, far_ref):
    unpack(packed_ref, 0, near_ref)
    unpack(packed_ref, 1, far_ref)
    later = near_ref[...] + times_wide(far_ref[...], factor_ref, 1)
    out_ref[...] = base_ref[...].astype(wide) + times_wide(later, factor_ref, 0)


def all_days(rows, factor_refs):
    for ref in factor_refs:
        for day in (1, 0):
            rows = times_wide(rows, ref, day)
    return rows


def step_out(rows_ref, *refs):
    pack(all_days(rows_ref[...], refs[:-1]), refs[-1], 0)


def step_in(packed_ref, base_ref, *refs):
    out_ref, rows_ref = refs[-2:]
    unpack(packed_ref, 0, rows_ref)
    out_ref[...] = base_ref[...] + all_days(rows_ref[...], refs[:-2])


def call(body, shape, scratch, operands, factors):
    vmem = pl.BlockSpec(memory_space=pltpu.VMEM)
    factors = [pltpu.with_memory_space_constraint(factor, pltpu.VMEM) for factor in factors]
    return pl.pallas_call(
        body,
        out_shape=jax.ShapeDtypeStruct(shape, wide),
        in_specs=[vmem] * (len(operands) + len(factors)),
        out_specs=vmem,
        scratch_shapes=[pltpu.VMEM(size, wide) for size in scratch],
        compiler_params=pltpu.CompilerParams(vmem_limit_bytes=VMEM_LIMIT),
    )(*operands, *factors)


def traded(value):
    return lax.all_to_all(value, ("row", "col"), 0, 0, tiled=True)


def product(left, right):
    return jnp.dot(left, right, preferred_element_type=wide)


def product_t(left, right):
    return lax.dot_general(left, right, (((0,), (0,)), ((), ())), preferred_element_type=wide)


def shards(inverse_blocks, factor_blocks, sigma_end):
    chips = lax.axis_size("col")
    days, rows, half = factor_blocks.shape
    nodes = chips * rows
    devices = 2 * chips
    core = lax.axis_index("row")
    chip = lax.axis_index("col")
    group = lax.axis_index("days")
    final_group = group == lax.axis_size("days") - 1

    fixed = jnp.stack([inverse_blocks[0], inverse_blocks[1], sigma_end])
    ahead, fixed_other = lax.optimization_barrier(
        (shifted(factor_blocks, 1), other_core(fixed))
    )
    next_mine = lax.all_gather(ahead, "col", axis=0)
    fixed = ordered(fixed, fixed_other, 2)
    mine = spread(factor_blocks)
    own = staged(mine, other_core(mine))

    strips = lax.dynamic_slice_in_dim(fixed, core * STRIP, STRIP, 1)
    base, last_strip, sigma_strip = (strips[0], strips[1], strips[2])
    started = jnp.where(final_group, sigma_strip, jnp.zeros_like(sigma_strip))

    strip_shape = (STRIP, nodes)
    packed = call(first_out, (devices, 2 * PACK, 128), [], [last_strip, started], [own])
    first_state = call(first_in, strip_shape, [strip_shape] * 2, [traded(packed), base], [own])

    def step(base, arrived, factors):
        packed = call(step_out, (devices, PACK, 128), [], [arrived], factors)
        return call(step_in, strip_shape, [strip_shape], [traded(packed), base], factors)

    even = range(2, lax.axis_size("days"), 2)
    state = step(first_state, shifted(first_state, 1), [own])
    pair_state, next_mine = lax.optimization_barrier((state, next_mine))
    following = staged(next_mine, other_core(next_mine))
    inverse_last = lax.all_gather(inverse_blocks[1], "col", axis=0)
    state = step(pair_state, shifted(pair_state, 2, even), [following, own])
    state = step(pair_state, shifted(state, 2, even), [following, own])
    state, inverse_last = lax.optimization_barrier((state, inverse_last))
    inverse_last_full = both_cores(inverse_last, 2).reshape(nodes, nodes)
    beside = shifted(state.astype(narrow), 1, even)
    state = step(shifted(first_state, 1), shifted(state, 2, even), [following])

    separator = jnp.where(group % 2 == 0, state.astype(narrow), beside)
    separator = jnp.where(final_group, sigma_strip, separator)
    strips = spread(separator)
    covariance = ordered(strips, other_core(strips), 1).reshape(nodes, nodes)

    factor_first, factor_last = (own[0].reshape(nodes, nodes), own[1].reshape(nodes, nodes))
    cross_last = product(covariance, factor_last).astype(narrow)
    marginal_last = (
        inverse_last_full.astype(wide) + product_t(factor_last, cross_last)
    ).astype(narrow)
    factor_first_half = mine[:, 0].reshape(nodes, half)
    cross_first_half = product(marginal_last, factor_first_half).astype(narrow)
    factor_first_rows = lax.dynamic_slice_in_dim(factor_first, chip * rows, rows, 1)
    marginal_first = (
        inverse_blocks[0].astype(wide) + product_t(factor_first_rows, cross_first_half)
    ).astype(narrow)

    def mine_of(value):
        return lax.dynamic_slice(value, (chip * rows, core * half), (rows, half))

    cross_first = lax.dynamic_slice_in_dim(cross_first_half, chip * rows, rows, 0)
    return (
        jnp.stack([marginal_first, mine_of(marginal_last)]),
        jnp.stack([cross_first, mine_of(cross_last)]),
    )


def solution(mesh):
    placed = (P("days", "col", "row"), P("days", "col", "row"), P("col", "row"))
    return jax.shard_map(
        shards,
        mesh=mesh,
        in_specs=placed,
        out_specs=(P("days", "col", "row"), P("days", "col", "row")),
        check_vma=False,
    )
```

```python
import functools

import jax
import jax.numpy as jnp
from jax import lax
from jax.experimental import pallas as pl
from jax.experimental.pallas import tpu as pltpu
from jax.sharding import PartitionSpec as P

narrow = jnp.bfloat16
wide = jnp.float32
STRIP = 32
PACK = 8
BLOCK = 256
SIDE = 4
VMEM_LIMIT = 20 * 1024 * 1024

vmem = pl.BlockSpec(memory_space=pltpu.VMEM)
hbm = pl.BlockSpec(memory_space=pltpu.HBM)


def params():
    return pltpu.CompilerParams(vmem_limit_bytes=VMEM_LIMIT)


def pinned(value):
    return pltpu.with_memory_space_constraint(value, pltpu.VMEM)


def outside(value):
    return pltpu.with_memory_space_constraint(value, pltpu.HBM)


def hop(value, steps, sources):
    return lax.ppermute(value, "days", [(source, source - steps) for source in sources])


def other_core(value):
    return lax.ppermute(value, "row", [(0, 1), (1, 0)])


def around(value, stride):
    count = lax.axis_size("col")
    return [
        lax.ppermute(
            value,
            "col",
            [
                (chip, chip + ((chip // stride + turn) % SIDE - chip // stride % SIDE) * stride)
                for chip in range(count)
            ],
        )
        for turn in range(1, SIDE)
    ]


def ordered(own, other, axis):
    first = lax.axis_index("row") == 0
    return jnp.concatenate([jnp.where(first, own, other), jnp.where(first, other, own)], axis=axis)


def to_chips(value):
    return lax.all_to_all(value, "col", 0, 0, tiled=True)


def to_devices(value):
    return lax.all_to_all(value, ("row", "col"), 0, 0, tiled=True)


def halves(value):
    high = value.astype(narrow)
    return (high, (value - high.astype(wide)).astype(narrow))


def whole(factor_ref, day):
    _, chips, rows, nodes = factor_ref.shape
    return factor_ref[day].reshape(chips * rows, nodes)


def times(pieces, factor_ref, day):
    return jnp.dot(pieces, whole(factor_ref, day), preferred_element_type=wide)


def times_wide(rows, factor_ref, day):
    split = times(jnp.concatenate(halves(rows), 0), factor_ref, day)
    count = rows.shape[0]
    return split[:count] + split[count:]


def all_days(rows, factor_refs):
    for ref in factor_refs:
        for day in range(ref.shape[0] - 1, -1, -1):
            rows = times_wide(rows, ref, day)
    return rows


def pack(rows, out_ref, place):
    devices = out_ref.shape[0]
    chips = devices // 2
    padded = jnp.concatenate([rows, jnp.zeros((128 - STRIP, rows.shape[1]), wide)], axis=0)
    turned = padded.T
    for core in range(2):
        for chip in range(chips):
            start = (2 * chip + core) * STRIP
            for part in range(STRIP // PACK):
                out_ref[
                    core * chips + chip,
                    place * PACK : (place + 1) * PACK,
                    part * STRIP : (part + 1) * STRIP,
                ] = turned[start + part * PACK : start + (part + 1) * PACK, :STRIP]


def unpack(in_ref, place, rows_ref):
    devices = in_ref.shape[0]
    chips = devices // 2
    for core in range(2):
        for chip in range(chips):
            start = (2 * chip + core) * STRIP
            for part in range(STRIP // PACK):
                rows_ref[part * PACK : (part + 1) * PACK, start : start + STRIP] = in_ref[
                    core * chips + chip,
                    place * PACK : (place + 1) * PACK,
                    part * STRIP : (part + 1) * STRIP,
                ]


def copied(value, chips):
    def body(in_ref, out_ref):
        for chip in range(chips):
            out_ref[chip] = in_ref[...]

    return pl.pallas_call(
        body,
        out_shape=jax.ShapeDtypeStruct((chips,) + value.shape, value.dtype),
        in_specs=[vmem],
        out_specs=vmem,
        compiler_params=params(),
    )(value)


def lined(own, others, stride):
    shape = own.shape

    def body(*refs):
        out_ref = refs[-1]
        place = lax.axis_index("col") // stride % SIDE
        for turn, ref in enumerate(refs[:-1]):
            source = (place + SIDE - turn) % SIDE
            out_ref[pl.ds(source * shape[0], shape[0])] = ref[...]

    return pl.pallas_call(
        body,
        out_shape=jax.ShapeDtypeStruct((SIDE * shape[0],) + shape[1:], own.dtype),
        in_specs=[vmem] * SIDE,
        out_specs=vmem,
        compiler_params=params(),
    )(own, *others)


def staged(own, other):
    days = len(own)
    chips, _, rows, half = own[0][0].shape
    layers = [layer for pair in zip(own, other) for _, layer in pair]

    def body(*refs):
        out_ref, sems = refs[-2:]
        core = lax.axis_index("row")
        copies = []
        for which, layer in enumerate(layers):
            place = core if which % 2 == 0 else 1 - core
            start = pl.multiple_of(place * half, half)
            copies.append(
                pltpu.make_async_copy(
                    refs[which].at[:, layer],
                    out_ref.at[which // 2, :, :, pl.ds(start, half)],
                    sems.at[which],
                )
            )
        for copy in copies:
            copy.start()
        for copy in copies:
            copy.wait()

    return pl.pallas_call(
        body,
        out_shape=pltpu.VMEM((days, chips, rows, 2 * half), narrow),
        in_specs=[hbm] * (2 * days),
        out_specs=vmem,
        scratch_shapes=[pltpu.SemaphoreType.DMA((2 * days,))],
        compiler_params=params(),
    )(*[value for pair in zip(own, other) for value, _ in pair])


def first_out(inverse_ref, sigma_ref, factor_ref, out_ref):
    later = times(sigma_ref[...], factor_ref, 1)
    stacked = jnp.concatenate([inverse_ref[...], *halves(later)], 0)
    split = times(stacked, factor_ref, 0)
    pack(split[:STRIP], out_ref, 0)
    pack(split[STRIP : 2 * STRIP] + split[2 * STRIP :], out_ref, 1)


def first_in(packed_ref, base_ref, factor_ref, out_ref, near_ref, far_ref):
    unpack(packed_ref, 0, near_ref)
    unpack(packed_ref, 1, far_ref)
    later = near_ref[...] + times_wide(far_ref[...], factor_ref, 1)
    out_ref[...] = base_ref[...].astype(wide) + times_wide(later, factor_ref, 0)


def step_out(rows_ref, *refs):
    pack(all_days(rows_ref[...], refs[:-1]), refs[-1], 0)


def step_in(packed_ref, base_ref, *refs):
    out_ref, rows_ref = refs[-2:]
    unpack(packed_ref, 0, rows_ref)
    out_ref[...] = base_ref[...] + all_days(rows_ref[...], refs[:-2])


def last_out(far_ref, next_ref, factor_ref, out_ref):
    part_way = all_days(far_ref[...], [next_ref])
    pack(part_way, out_ref, 0)
    pack(all_days(part_way, [factor_ref]), out_ref, 1)


def last_in(
    packed_ref,
    near_ref,
    state_ref,
    sigma_ref,
    next_ref,
    factor_ref,
    kept_ref,
    out_ref,
    first_ref,
    second_ref,
):
    unpack(packed_ref, 0, first_ref)
    unpack(packed_ref, 1, second_ref)
    stacked = all_days(jnp.concatenate([first_ref[...], second_ref[...]], 0), [next_ref])
    kept = (near_ref[...] + stacked[:STRIP]).astype(narrow)
    final_group = lax.axis_index("days") == lax.axis_size("days") - 1
    kept_ref[...] = jnp.where(final_group, sigma_ref[...], kept)
    before = state_ref[...] + all_days(stacked[STRIP:], [factor_ref])
    out_ref[...] = before.astype(narrow)


def chosen(kept_ref, arrived_ref, out_ref):
    group = lax.axis_index("days")
    keep = (group == 1) | (group == 3) | (group == lax.axis_size("days") - 1)
    separator = jnp.where(keep, kept_ref[...], arrived_ref[...])
    for chip in range(out_ref.shape[0]):
        out_ref[chip] = separator


def inner_days(
    own_ref,
    other_ref,
    factor_ref,
    inverse_own_ref,
    inverse_other_ref,
    inverse_first_ref,
    marginal_ref,
    cross_ref,
    covariance_ref,
    cross_last_ref,
    marginal_last_ref,
    cross_first_ref,
):
    core = lax.axis_index("row")
    chip = lax.axis_index("col")
    _, chips, rows, nodes = factor_ref.shape
    half = nodes // 2
    for place in range(chips):
        for ref, which in ((own_ref, core), (other_ref, 1 - core)):
            start = pl.multiple_of(place * rows + which * STRIP, STRIP)
            covariance_ref[pl.ds(start, STRIP)] = ref[place]
    for start in range(0, nodes, BLOCK):
        cross_last_ref[start : start + BLOCK] = times(
            covariance_ref[start : start + BLOCK], factor_ref, 1
        ).astype(narrow)
    for block in range(nodes // BLOCK):
        start = block * BLOCK
        factor_cols = factor_ref[1, :, :, start : start + BLOCK].reshape(nodes, BLOCK)
        summed = lax.dot_general(
            factor_cols,
            cross_last_ref[...],
            (((0,), (0,)), ((), ())),
            preferred_element_type=wide,
        )
        layers = slice(start // rows, (start + BLOCK) // rows)
        own = inverse_own_ref[layers].reshape(BLOCK, half)
        other = inverse_other_ref[layers].reshape(BLOCK, half)
        left = jnp.where(core == 0, own, other).astype(wide) + summed[:, :half]
        right = jnp.where(core == 0, other, own).astype(wide) + summed[:, half:]
        marginal_last_ref[start : start + BLOCK, :half] = left.astype(narrow)
        marginal_last_ref[start : start + BLOCK, half:] = right.astype(narrow)
    columns = pl.ds(pl.multiple_of(core * half, half), half)
    first_half = factor_ref[0, :, :, columns].reshape(nodes, half)
    for start in range(0, nodes, BLOCK):
        cross_first_ref[start : start + BLOCK] = jnp.dot(
            marginal_last_ref[start : start + BLOCK], first_half, preferred_element_type=wide
        ).astype(narrow)
    near = pl.ds(pl.multiple_of((chip // 2) * 2 * rows, 2 * rows), 2 * rows)
    summed = lax.dot_general(
        factor_ref[0, :, :, near].reshape(nodes, 2 * rows),
        cross_first_ref[...],
        (((0,), (0,)), ((), ())),
        preferred_element_type=wide,
    )
    summed = jnp.where(chip % 2 == 0, summed[:rows], summed[rows:])
    mine = pl.ds(pl.multiple_of(chip * rows, rows), rows)
    marginal_ref[0] = (inverse_first_ref[...].astype(wide) + summed).astype(narrow)
    marginal_ref[1] = marginal_last_ref[mine, columns]
    cross_ref[0] = cross_first_ref[mine]
    cross_ref[1] = cross_last_ref[mine, columns]


def call(body, outs, scratch, operands, factors):
    single = not isinstance(outs, list)
    return pl.pallas_call(
        body,
        out_shape=outs if single else tuple(outs),
        in_specs=[vmem] * (len(operands) + len(factors)),
        out_specs=vmem if single else tuple([vmem] * len(outs)),
        scratch_shapes=scratch,
        compiler_params=params(),
    )(*operands, *[pinned(factor) for factor in factors])


def shards(inverse_blocks, factor_blocks, sigma_end):
    chips = lax.axis_size("col")
    days, rows, half = factor_blocks.shape
    nodes = chips * rows
    devices = 2 * chips
    core = lax.axis_index("row")
    final_group = lax.axis_index("days") == lax.axis_size("days") - 1

    fixed = jnp.stack([inverse_blocks[0], inverse_blocks[1], sigma_end])
    fixed = ordered(fixed, other_core(fixed), 2)
    strips = lax.dynamic_slice_in_dim(fixed, core * STRIP, STRIP, 1)
    base, last_strip, sigma_strip = (strips[0], strips[1], strips[2])
    started = jnp.where(final_group, sigma_strip, jnp.zeros_like(sigma_strip))

    mine = to_chips(copied(factor_blocks, chips))
    inverse_last = inverse_blocks[1:]
    inverse_line = lined(inverse_last, around(inverse_last, 1), 1)
    (mine, mine_first, mine_last, inverse_line, base, last_strip, sigma_strip, started) = (
        lax.optimization_barrier(
            (
                mine,
                mine[:, :1],
                mine[:, 1:],
                inverse_line,
                base,
                last_strip,
                sigma_strip,
                started,
            )
        )
    )
    next_last = hop(mine_last, 1, (2, 4))
    theirs = other_core(mine)
    own = staged([(mine, 0), (mine, 1)], [(theirs, 0), (theirs, 1)])

    strip = (STRIP, nodes)
    state_shape = jax.ShapeDtypeStruct(strip, wide)
    rows_scratch = pltpu.VMEM(strip, wide)

    def packed_shape(count):
        return jax.ShapeDtypeStruct((devices, count * PACK, 128), wide)

    packed = call(first_out, packed_shape(2), [], [last_strip, started], [own])
    first_state = call(
        first_in, state_shape, [rows_scratch] * 2, [to_devices(packed), base], [own]
    )

    def step(base, arrived, factors):
        packed = call(step_out, packed_shape(1), [], [arrived], factors)
        return call(
            step_in, state_shape, [rows_scratch], [to_devices(packed), base], factors
        )

    near, mine_first, next_last = lax.optimization_barrier(
        (hop(first_state, 1, (2, 4, 7)), mine_first, next_last)
    )
    next_first = hop(mine_first, 1, (2, 4))
    state = step(first_state, near, [own])
    state = step(state, hop(state, 1, (6,)), [own])

    pair_state, next_first, beside = lax.optimization_barrier(
        (state, next_first, around(inverse_line, SIDE))
    )
    far = hop(pair_state, 2, (5,))
    inverse_mine = lined(inverse_line, beside, SIDE)
    following = staged(
        [(outside(next_first), 0), (outside(next_last), 0)],
        [(outside(other_core(next_first)), 0), (outside(other_core(next_last)), 0)],
    )
    factors = [following, own]
    state = step(pair_state, far, factors)
    far, inverse_theirs = lax.optimization_barrier(
        (hop(state, 2, (3, 5)), other_core(inverse_mine))
    )
    packed = call(last_out, packed_shape(2), [], [far], factors)
    strip_narrow = jax.ShapeDtypeStruct(strip, narrow)
    kept, before = call(
        last_in,
        [strip_narrow, strip_narrow],
        [rows_scratch] * 2,
        [to_devices(packed), near, pair_state, sigma_strip],
        factors,
    )
    copies = call(
        chosen,
        jax.ShapeDtypeStruct((chips,) + strip, narrow),
        [],
        [kept, hop(before, 1, (1, 3, 5, 6, 7))],
        [],
    )
    separator = to_chips(copies)
    block = jax.ShapeDtypeStruct((days, rows, half), narrow)
    square = pltpu.VMEM((nodes, nodes), narrow)
    return pl.pallas_call(
        inner_days,
        out_shape=(block, block),
        in_specs=[vmem] * 6,
        out_specs=(vmem, vmem),
        scratch_shapes=[square] * 3 + [pltpu.VMEM((nodes, half), narrow)],
        compiler_params=params(),
    )(
        separator,
        other_core(separator),
        pinned(own),
        inverse_mine,
        inverse_theirs,
        inverse_blocks[0],
    )


def solution(mesh):
    placed = (P("days", "col", "row"), P("days", "col", "row"), P("col", "row"))
    return jax.shard_map(
        shards,
        mesh=mesh,
        in_specs=placed,
        out_specs=(P("days", "col", "row"), P("days", "col", "row")),
        check_vma=False,
    )
```

```python
import functools

import jax
import jax.numpy as jnp
from jax import lax
from jax.experimental import pallas as pl
from jax.experimental.pallas import tpu as pltpu
from jax.sharding import PartitionSpec as P

narrow = jnp.bfloat16
wide = jnp.float32
STRIP = 32
PACK = 8
BLOCK = 256
SIDE = 4
VMEM_LIMIT = 20 * 1024 * 1024

vmem = pl.BlockSpec(memory_space=pltpu.VMEM)
hbm = pl.BlockSpec(memory_space=pltpu.HBM)


def params():
    return pltpu.CompilerParams(vmem_limit_bytes=VMEM_LIMIT)


def pinned(value):
    return pltpu.with_memory_space_constraint(value, pltpu.VMEM)


def outside(value):
    return pltpu.with_memory_space_constraint(value, pltpu.HBM)


def hop(value, steps, sources):
    return lax.ppermute(value, "days", [(source, source - steps) for source in sources])


def other_core(value):
    return lax.ppermute(value, "row", [(0, 1), (1, 0)])


def around(value, stride):
    count = lax.axis_size("col")
    return [
        lax.ppermute(
            value,
            "col",
            [
                (chip, chip + ((chip // stride + turn) % SIDE - chip // stride % SIDE) * stride)
                for chip in range(count)
            ],
        )
        for turn in range(1, SIDE)
    ]


def ordered(own, other, axis):
    first = lax.axis_index("row") == 0
    return jnp.concatenate([jnp.where(first, own, other), jnp.where(first, other, own)], axis=axis)


def to_chips(value):
    return lax.all_to_all(value, "col", 0, 0, tiled=True)


def to_devices(value):
    return lax.all_to_all(value, ("row", "col"), 0, 0, tiled=True)


def halves(value):
    high = value.astype(narrow)
    return (high, (value - high.astype(wide)).astype(narrow))


def whole(factor_ref, day):
    _, chips, rows, nodes = factor_ref.shape
    return factor_ref[day].reshape(chips * rows, nodes)


def times(pieces, factor_ref, day):
    return jnp.dot(pieces, whole(factor_ref, day), preferred_element_type=wide)


def times_wide(rows, factor_ref, day):
    split = times(jnp.concatenate(halves(rows), 0), factor_ref, day)
    count = rows.shape[0]
    return split[:count] + split[count:]


def all_days(rows, factor_refs):
    for ref in factor_refs:
        for day in range(ref.shape[0] - 1, -1, -1):
            rows = times_wide(rows, ref, day)
    return rows


def pack(rows, out_ref, place):
    devices = out_ref.shape[0]
    chips = devices // 2
    padded = jnp.concatenate([rows, jnp.zeros((128 - STRIP, rows.shape[1]), wide)], axis=0)
    turned = padded.T
    for core in range(2):
        for chip in range(chips):
            start = (2 * chip + core) * STRIP
            for part in range(STRIP // PACK):
                out_ref[
                    core * chips + chip,
                    place * PACK : (place + 1) * PACK,
                    part * STRIP : (part + 1) * STRIP,
                ] = turned[start + part * PACK : start + (part + 1) * PACK, :STRIP]


def unpack(in_ref, place, rows_ref):
    devices = in_ref.shape[0]
    chips = devices // 2
    for core in range(2):
        for chip in range(chips):
            start = (2 * chip + core) * STRIP
            for part in range(STRIP // PACK):
                rows_ref[part * PACK : (part + 1) * PACK, start : start + STRIP] = in_ref[
                    core * chips + chip,
                    place * PACK : (place + 1) * PACK,
                    part * STRIP : (part + 1) * STRIP,
                ]


def copied(value, chips):
    def body(in_ref, out_ref):
        for chip in range(chips):
            out_ref[chip] = in_ref[...]

    return pl.pallas_call(
        body,
        out_shape=jax.ShapeDtypeStruct((chips,) + value.shape, value.dtype),
        in_specs=[vmem],
        out_specs=vmem,
        compiler_params=params(),
    )(value)


def lined(own, others, stride):
    shape = own.shape

    def body(*refs):
        out_ref = refs[-1]
        place = lax.axis_index("col") // stride % SIDE
        for turn, ref in enumerate(refs[:-1]):
            source = (place + SIDE - turn) % SIDE
            out_ref[pl.ds(source * shape[0], shape[0])] = ref[...]

    return pl.pallas_call(
        body,
        out_shape=jax.ShapeDtypeStruct((SIDE * shape[0],) + shape[1:], own.dtype),
        in_specs=[vmem] * SIDE,
        out_specs=vmem,
        compiler_params=params(),
    )(own, *others)


def staged(own, other):
    days = len(own)
    chips, _, rows, half = own[0][0].shape
    layers = [layer for pair in zip(own, other) for _, layer in pair]

    def body(*refs):
        out_ref, sems = refs[-2:]
        core = lax.axis_index("row")
        copies = []
        for which, layer in enumerate(layers):
            place = core if which % 2 == 0 else 1 - core
            start = pl.multiple_of(place * half, half)
            copies.append(
                pltpu.make_async_copy(
                    refs[which].at[:, layer],
                    out_ref.at[which // 2, :, :, pl.ds(start, half)],
                    sems.at[which],
                )
            )
        for copy in copies:
            copy.start()
        for copy in copies:
            copy.wait()

    return pl.pallas_call(
        body,
        out_shape=pltpu.VMEM((days, chips, rows, 2 * half), narrow),
        in_specs=[hbm] * (2 * days),
        out_specs=vmem,
        scratch_shapes=[pltpu.SemaphoreType.DMA((2 * days,))],
        compiler_params=params(),
    )(*[value for pair in zip(own, other) for value, _ in pair])


def first_out(inverse_ref, sigma_ref, factor_ref, out_ref):
    later = times(sigma_ref[...], factor_ref, 1)
    stacked = jnp.concatenate([inverse_ref[...], *halves(later)], 0)
    split = times(stacked, factor_ref, 0)
    pack(split[:STRIP], out_ref, 0)
    pack(split[STRIP : 2 * STRIP] + split[2 * STRIP :], out_ref, 1)


def first_in(packed_ref, base_ref, factor_ref, out_ref, near_ref, far_ref):
    unpack(packed_ref, 0, near_ref)
    unpack(packed_ref, 1, far_ref)
    later = near_ref[...] + times_wide(far_ref[...], factor_ref, 1)
    out_ref[...] = base_ref[...].astype(wide) + times_wide(later, factor_ref, 0)


def step_out(rows_ref, *refs):
    pack(all_days(rows_ref[...], refs[:-1]), refs[-1], 0)


def step_in(packed_ref, base_ref, *refs):
    out_ref, rows_ref = refs[-2:]
    unpack(packed_ref, 0, rows_ref)
    out_ref[...] = base_ref[...] + all_days(rows_ref[...], refs[:-2])


def last_out(far_ref, next_ref, factor_ref, out_ref):
    part_way = all_days(far_ref[...], [next_ref])
    pack(part_way, out_ref, 0)
    pack(all_days(part_way, [factor_ref]), out_ref, 1)


def last_in(
    packed_ref,
    near_ref,
    state_ref,
    sigma_ref,
    next_ref,
    factor_ref,
    kept_ref,
    out_ref,
    first_ref,
    second_ref,
):
    unpack(packed_ref, 0, first_ref)
    unpack(packed_ref, 1, second_ref)
    stacked = all_days(jnp.concatenate([first_ref[...], second_ref[...]], 0), [next_ref])
    kept = (near_ref[...] + stacked[:STRIP]).astype(narrow)
    final_group = lax.axis_index("days") == lax.axis_size("days") - 1
    kept_ref[...] = jnp.where(final_group, sigma_ref[...], kept)
    before = state_ref[...] + all_days(stacked[STRIP:], [factor_ref])
    out_ref[...] = before.astype(narrow)


def chosen(kept_ref, arrived_ref, out_ref):
    group = lax.axis_index("days")
    keep = (group == 1) | (group == 3) | (group == lax.axis_size("days") - 1)
    separator = jnp.where(keep, kept_ref[...], arrived_ref[...])
    for chip in range(out_ref.shape[0]):
        out_ref[chip] = separator


def inner_days(
    own_ref,
    other_ref,
    factor_ref,
    inverse_own_ref,
    inverse_other_ref,
    inverse_first_ref,
    marginal_ref,
    cross_ref,
    covariance_ref,
    cross_last_ref,
    marginal_last_ref,
    cross_first_ref,
):
    core = lax.axis_index("row")
    chip = lax.axis_index("col")
    _, chips, rows, nodes = factor_ref.shape
    half = nodes // 2
    for place in range(chips):
        for ref, which in ((own_ref, core), (other_ref, 1 - core)):
            start = pl.multiple_of(place * rows + which * STRIP, STRIP)
            covariance_ref[pl.ds(start, STRIP)] = ref[place]
    for start in range(0, nodes, BLOCK):
        cross_last_ref[start : start + BLOCK] = times(
            covariance_ref[start : start + BLOCK], factor_ref, 1
        ).astype(narrow)
    for block in range(nodes // BLOCK):
        start = block * BLOCK
        factor_cols = factor_ref[1, :, :, start : start + BLOCK].reshape(nodes, BLOCK)
        summed = lax.dot_general(
            factor_cols,
            cross_last_ref[...],
            (((0,), (0,)), ((), ())),
            preferred_element_type=wide,
        )
        layers = slice(start // rows, (start + BLOCK) // rows)
        own = inverse_own_ref[layers].reshape(BLOCK, half)
        other = inverse_other_ref[layers].reshape(BLOCK, half)
        left = jnp.where(core == 0, own, other).astype(wide) + summed[:, :half]
        right = jnp.where(core == 0, other, own).astype(wide) + summed[:, half:]
        marginal_last_ref[start : start + BLOCK, :half] = left.astype(narrow)
        marginal_last_ref[start : start + BLOCK, half:] = right.astype(narrow)
    columns = pl.ds(pl.multiple_of(core * half, half), half)
    first_half = factor_ref[0, :, :, columns].reshape(nodes, half)
    for start in range(0, nodes, BLOCK):
        cross_first_ref[start : start + BLOCK] = jnp.dot(
            marginal_last_ref[start : start + BLOCK], first_half, preferred_element_type=wide
        ).astype(narrow)
    near = pl.ds(pl.multiple_of((chip // 2) * 2 * rows, 2 * rows), 2 * rows)
    summed = lax.dot_general(
        factor_ref[0, :, :, near].reshape(nodes, 2 * rows),
        cross_first_ref[...],
        (((0,), (0,)), ((), ())),
        preferred_element_type=wide,
    )
    summed = jnp.where(chip % 2 == 0, summed[:rows], summed[rows:])
    mine = pl.ds(pl.multiple_of(chip * rows, rows), rows)
    marginal_ref[0] = (inverse_first_ref[...].astype(wide) + summed).astype(narrow)
    marginal_ref[1] = marginal_last_ref[mine, columns]
    cross_ref[0] = cross_first_ref[mine]
    cross_ref[1] = cross_last_ref[mine, columns]


def call(body, outs, scratch, operands, factors):
    single = not isinstance(outs, list)
    return pl.pallas_call(
        body,
        out_shape=outs if single else tuple(outs),
        in_specs=[vmem] * (len(operands) + len(factors)),
        out_specs=vmem if single else tuple([vmem] * len(outs)),
        scratch_shapes=scratch,
        compiler_params=params(),
    )(*operands, *[pinned(factor) for factor in factors])


def shards(inverse_blocks, factor_blocks, sigma_end):
    chips = lax.axis_size("col")
    days, rows, half = factor_blocks.shape
    nodes = chips * rows
    devices = 2 * chips
    core = lax.axis_index("row")
    final_group = lax.axis_index("days") == lax.axis_size("days") - 1

    fixed = jnp.stack([inverse_blocks[0], inverse_blocks[1], sigma_end])
    fixed = ordered(fixed, other_core(fixed), 2)
    strips = lax.dynamic_slice_in_dim(fixed, core * STRIP, STRIP, 1)
    base, last_strip, sigma_strip = (strips[0], strips[1], strips[2])
    started = jnp.where(final_group, sigma_strip, jnp.zeros_like(sigma_strip))

    mine = to_chips(copied(factor_blocks, chips))
    inverse_last = inverse_blocks[1:]
    inverse_line = lined(inverse_last, around(inverse_last, 1), 1)
    (mine, mine_first, mine_last, inverse_line, base, last_strip, sigma_strip, started) = (
        lax.optimization_barrier(
            (
                mine,
                mine[:, :1],
                mine[:, 1:],
                inverse_line,
                base,
                last_strip,
                sigma_strip,
                started,
            )
        )
    )
    next_last = hop(mine_last, 1, (2, 4))
    theirs = other_core(mine)
    own = staged([(mine, 0), (mine, 1)], [(theirs, 0), (theirs, 1)])

    strip = (STRIP, nodes)
    state_shape = jax.ShapeDtypeStruct(strip, wide)
    rows_scratch = pltpu.VMEM(strip, wide)

    def packed_shape(count):
        return jax.ShapeDtypeStruct((devices, count * PACK, 128), wide)

    packed = call(first_out, packed_shape(2), [], [last_strip, started], [own])
    first_state = call(
        first_in, state_shape, [rows_scratch] * 2, [to_devices(packed), base], [own]
    )

    def step(base, arrived, factors):
        packed = call(step_out, packed_shape(1), [], [arrived], factors)
        return call(
            step_in, state_shape, [rows_scratch], [to_devices(packed), base], factors
        )

    near, mine_first, next_last = lax.optimization_barrier(
        (hop(first_state, 1, (2, 4, 7)), mine_first, next_last)
    )
    next_first = hop(mine_first, 1, (2, 4))
    state = step(first_state, near, [own])
    state = step(state, hop(state, 1, (6,)), [own])

    pair_state, next_first, next_last, beside = lax.optimization_barrier(
        (state, next_first, next_last, around(inverse_line, SIDE))
    )
    far = hop(pair_state, 2, (5,))
    inverse_mine = lined(inverse_line, beside, SIDE)
    following = staged(
        [(outside(next_first), 0), (outside(next_last), 0)],
        [(outside(other_core(next_first)), 0), (outside(other_core(next_last)), 0)],
    )
    factors = [following, own]
    state = step(pair_state, far, factors)
    far, inverse_theirs = lax.optimization_barrier(
        (hop(state, 2, (3, 5)), other_core(inverse_mine))
    )
    packed = call(last_out, packed_shape(2), [], [far], factors)
    strip_narrow = jax.ShapeDtypeStruct(strip, narrow)
    kept, before = call(
        last_in,
        [strip_narrow, strip_narrow],
        [rows_scratch] * 2,
        [to_devices(packed), near, pair_state, sigma_strip],
        factors,
    )
    copies = call(
        chosen,
        jax.ShapeDtypeStruct((chips,) + strip, narrow),
        [],
        [kept, hop(before, 1, (1, 3, 5, 6, 7))],
        [],
    )
    separator = to_chips(copies)
    block = jax.ShapeDtypeStruct((days, rows, half), narrow)
    square = pltpu.VMEM((nodes, nodes), narrow)
    return pl.pallas_call(
        inner_days,
        out_shape=(block, block),
        in_specs=[vmem] * 6,
        out_specs=(vmem, vmem),
        scratch_shapes=[square] * 3 + [pltpu.VMEM((nodes, half), narrow)],
        compiler_params=params(),
    )(
        separator,
        other_core(separator),
        pinned(own),
        inverse_mine,
        inverse_theirs,
        inverse_blocks[0],
    )


def solution(mesh):
    placed = (P("days", "col", "row"), P("days", "col", "row"), P("col", "row"))
    return jax.shard_map(
        shards,
        mesh=mesh,
        in_specs=placed,
        out_specs=(P("days", "col", "row"), P("days", "col", "row")),
        check_vma=False,
    )
```

```python
import functools

import jax
import jax.numpy as jnp
from jax import lax
from jax.experimental import pallas as pl
from jax.experimental.pallas import tpu as pltpu
from jax.sharding import PartitionSpec as P

narrow = jnp.bfloat16
wide = jnp.float32
STRIP = 32
PACK = 8
BLOCK = 256
SIDE = 4
VMEM_LIMIT = 20 * 1024 * 1024

vmem = pl.BlockSpec(memory_space=pltpu.VMEM)
hbm = pl.BlockSpec(memory_space=pltpu.HBM)


def params():
    return pltpu.CompilerParams(vmem_limit_bytes=VMEM_LIMIT)


def pinned(value):
    return pltpu.with_memory_space_constraint(value, pltpu.VMEM)


def outside(value):
    return pltpu.with_memory_space_constraint(value, pltpu.HBM)


def hop(value, steps, sources):
    return lax.ppermute(value, "days", [(source, source - steps) for source in sources])


def other_core(value):
    return lax.ppermute(value, "row", [(0, 1), (1, 0)])


def around(value, stride):
    count = lax.axis_size("col")
    return [
        lax.ppermute(
            value,
            "col",
            [
                (chip, chip + ((chip // stride + turn) % SIDE - chip // stride % SIDE) * stride)
                for chip in range(count)
            ],
        )
        for turn in range(1, SIDE)
    ]


def ordered(own, other, axis):
    first = lax.axis_index("row") == 0
    return jnp.concatenate([jnp.where(first, own, other), jnp.where(first, other, own)], axis=axis)


def to_chips(value):
    return lax.all_to_all(value, "col", 0, 0, tiled=True)


def to_devices(value):
    return lax.all_to_all(value, ("row", "col"), 0, 0, tiled=True)


def halves(value):
    high = value.astype(narrow)
    return (high, (value - high.astype(wide)).astype(narrow))


def whole(factor_ref, day):
    _, chips, rows, nodes = factor_ref.shape
    return factor_ref[day].reshape(chips * rows, nodes)


def times(pieces, factor_ref, day):
    return jnp.dot(pieces, whole(factor_ref, day), preferred_element_type=wide)


def times_wide(rows, factor_ref, day):
    split = times(jnp.concatenate(halves(rows), 0), factor_ref, day)
    count = rows.shape[0]
    return split[:count] + split[count:]


def all_days(rows, factor_refs):
    for ref in factor_refs:
        for day in range(ref.shape[0] - 1, -1, -1):
            rows = times_wide(rows, ref, day)
    return rows


def pack(rows, out_ref, place):
    devices = out_ref.shape[0]
    chips = devices // 2
    padded = jnp.concatenate([rows, jnp.zeros((128 - STRIP, rows.shape[1]), wide)], axis=0)
    turned = padded.T
    for core in range(2):
        for chip in range(chips):
            start = (2 * chip + core) * STRIP
            for part in range(STRIP // PACK):
                out_ref[
                    core * chips + chip,
                    place * PACK : (place + 1) * PACK,
                    part * STRIP : (part + 1) * STRIP,
                ] = turned[start + part * PACK : start + (part + 1) * PACK, :STRIP]


def unpack(in_ref, place, rows_ref):
    devices = in_ref.shape[0]
    chips = devices // 2
    for core in range(2):
        for chip in range(chips):
            start = (2 * chip + core) * STRIP
            for part in range(STRIP // PACK):
                rows_ref[part * PACK : (part + 1) * PACK, start : start + STRIP] = in_ref[
                    core * chips + chip,
                    place * PACK : (place + 1) * PACK,
                    part * STRIP : (part + 1) * STRIP,
                ]


def copied(value, chips):
    def body(in_ref, out_ref):
        for chip in range(chips):
            out_ref[chip] = in_ref[...]

    return pl.pallas_call(
        body,
        out_shape=jax.ShapeDtypeStruct((chips,) + value.shape, value.dtype),
        in_specs=[vmem],
        out_specs=vmem,
        compiler_params=params(),
    )(value)


def lined(own, others, stride):
    shape = own.shape

    def body(*refs):
        out_ref = refs[-1]
        place = lax.axis_index("col") // stride % SIDE
        for turn, ref in enumerate(refs[:-1]):
            source = (place + SIDE - turn) % SIDE
            out_ref[pl.ds(source * shape[0], shape[0])] = ref[...]

    return pl.pallas_call(
        body,
        out_shape=jax.ShapeDtypeStruct((SIDE * shape[0],) + shape[1:], own.dtype),
        in_specs=[vmem] * SIDE,
        out_specs=vmem,
        compiler_params=params(),
    )(own, *others)


def staged(own, other):
    days = len(own)
    chips, _, rows, half = own[0][0].shape
    layers = [layer for pair in zip(own, other) for _, layer in pair]

    def body(*refs):
        out_ref, sems = refs[-2:]
        core = lax.axis_index("row")
        copies = []
        for which, layer in enumerate(layers):
            place = core if which % 2 == 0 else 1 - core
            start = pl.multiple_of(place * half, half)
            copies.append(
                pltpu.make_async_copy(
                    refs[which].at[:, layer],
                    out_ref.at[which // 2, :, :, pl.ds(start, half)],
                    sems.at[which],
                )
            )
        for copy in copies:
            copy.start()
        for copy in copies:
            copy.wait()

    return pl.pallas_call(
        body,
        out_shape=pltpu.VMEM((days, chips, rows, 2 * half), narrow),
        in_specs=[hbm] * (2 * days),
        out_specs=vmem,
        scratch_shapes=[pltpu.SemaphoreType.DMA((2 * days,))],
        compiler_params=params(),
    )(*[value for pair in zip(own, other) for value, _ in pair])


def first_out(inverse_ref, sigma_ref, factor_ref, out_ref):
    later = times(sigma_ref[...], factor_ref, 1)
    stacked = jnp.concatenate([inverse_ref[...], *halves(later)], 0)
    split = times(stacked, factor_ref, 0)
    pack(split[:STRIP], out_ref, 0)
    pack(split[STRIP : 2 * STRIP] + split[2 * STRIP :], out_ref, 1)


def first_in(packed_ref, base_ref, factor_ref, out_ref, near_ref, far_ref):
    unpack(packed_ref, 0, near_ref)
    unpack(packed_ref, 1, far_ref)
    later = near_ref[...] + times_wide(far_ref[...], factor_ref, 1)
    out_ref[...] = base_ref[...].astype(wide) + times_wide(later, factor_ref, 0)


def step_out(rows_ref, *refs):
    pack(all_days(rows_ref[...], refs[:-1]), refs[-1], 0)


def step_in(packed_ref, base_ref, *refs):
    out_ref, rows_ref = refs[-2:]
    unpack(packed_ref, 0, rows_ref)
    out_ref[...] = base_ref[...] + all_days(rows_ref[...], refs[:-2])


def last_out(far_ref, next_ref, factor_ref, out_ref):
    part_way = all_days(far_ref[...], [next_ref])
    pack(part_way, out_ref, 0)
    pack(all_days(part_way, [factor_ref]), out_ref, 1)


def last_in(
    packed_ref,
    near_ref,
    state_ref,
    sigma_ref,
    next_ref,
    factor_ref,
    kept_ref,
    out_ref,
    first_ref,
    second_ref,
):
    unpack(packed_ref, 0, first_ref)
    unpack(packed_ref, 1, second_ref)
    stacked = all_days(jnp.concatenate([first_ref[...], second_ref[...]], 0), [next_ref])
    kept = (near_ref[...] + stacked[:STRIP]).astype(narrow)
    final_group = lax.axis_index("days") == lax.axis_size("days") - 1
    kept_ref[...] = jnp.where(final_group, sigma_ref[...], kept)
    before = state_ref[...] + all_days(stacked[STRIP:], [factor_ref])
    out_ref[...] = before.astype(narrow)


def chosen(kept_ref, arrived_ref, out_ref):
    group = lax.axis_index("days")
    keep = (group == 1) | (group == 3) | (group == lax.axis_size("days") - 1)
    separator = jnp.where(keep, kept_ref[...], arrived_ref[...])
    for chip in range(out_ref.shape[0]):
        out_ref[chip] = separator


def own_rows(own_ref, factor_ref, out_ref):
    chips, strip, nodes = own_ref.shape
    rows = own_ref[...].reshape(chips * strip, nodes)
    for start in range(0, chips * strip, BLOCK):
        out_ref[start : start + BLOCK] = times(
            rows[start : start + BLOCK], factor_ref, 1
        ).astype(narrow)


def inner_days(
    own_ref,
    other_ref,
    factor_ref,
    inverse_own_ref,
    inverse_other_ref,
    inverse_first_ref,
    marginal_ref,
    cross_ref,
    covariance_ref,
    cross_last_ref,
    marginal_last_ref,
    cross_first_ref,
):
    core = lax.axis_index("row")
    chip = lax.axis_index("col")
    _, chips, rows, nodes = factor_ref.shape
    half = nodes // 2
    strips = other_ref[...].reshape(chips * STRIP, nodes)
    for start in range(0, chips * STRIP, BLOCK):
        covariance_ref[start : start + BLOCK] = times(
            strips[start : start + BLOCK], factor_ref, 1
        ).astype(narrow)
    for place in range(chips):
        for ref, which in ((own_ref, core), (covariance_ref, 1 - core)):
            start = pl.multiple_of(place * rows + which * STRIP, STRIP)
            cross_last_ref[pl.ds(start, STRIP)] = ref[place * STRIP : (place + 1) * STRIP]
    for block in range(nodes // BLOCK):
        start = block * BLOCK
        factor_cols = factor_ref[1, :, :, start : start + BLOCK].reshape(nodes, BLOCK)
        summed = lax.dot_general(
            factor_cols,
            cross_last_ref[...],
            (((0,), (0,)), ((), ())),
            preferred_element_type=wide,
        )
        layers = slice(start // rows, (start + BLOCK) // rows)
        own = inverse_own_ref[layers].reshape(BLOCK, half)
        other = inverse_other_ref[layers].reshape(BLOCK, half)
        left = jnp.where(core == 0, own, other).astype(wide) + summed[:, :half]
        right = jnp.where(core == 0, other, own).astype(wide) + summed[:, half:]
        marginal_last_ref[start : start + BLOCK, :half] = left.astype(narrow)
        marginal_last_ref[start : start + BLOCK, half:] = right.astype(narrow)
    columns = pl.ds(pl.multiple_of(core * half, half), half)
    first_half = factor_ref[0, :, :, columns].reshape(nodes, half)
    for start in range(0, nodes, BLOCK):
        cross_first_ref[start : start + BLOCK] = jnp.dot(
            marginal_last_ref[start : start + BLOCK], first_half, preferred_element_type=wide
        ).astype(narrow)
    near = pl.ds(pl.multiple_of((chip // 2) * 2 * rows, 2 * rows), 2 * rows)
    summed = lax.dot_general(
        factor_ref[0, :, :, near].reshape(nodes, 2 * rows),
        cross_first_ref[...],
        (((0,), (0,)), ((), ())),
        preferred_element_type=wide,
    )
    summed = jnp.where(chip % 2 == 0, summed[:rows], summed[rows:])
    mine = pl.ds(pl.multiple_of(chip * rows, rows), rows)
    marginal_ref[0] = (inverse_first_ref[...].astype(wide) + summed).astype(narrow)
    marginal_ref[1] = marginal_last_ref[mine, columns]
    cross_ref[0] = cross_first_ref[mine]
    cross_ref[1] = cross_last_ref[mine, columns]


def call(body, outs, scratch, operands, factors):
    single = not isinstance(outs, list)
    return pl.pallas_call(
        body,
        out_shape=outs if single else tuple(outs),
        in_specs=[vmem] * (len(operands) + len(factors)),
        out_specs=vmem if single else tuple([vmem] * len(outs)),
        scratch_shapes=scratch,
        compiler_params=params(),
    )(*operands, *[pinned(factor) for factor in factors])


def shards(inverse_blocks, factor_blocks, sigma_end):
    chips = lax.axis_size("col")
    days, rows, half = factor_blocks.shape
    nodes = chips * rows
    devices = 2 * chips
    core = lax.axis_index("row")
    final_group = lax.axis_index("days") == lax.axis_size("days") - 1

    fixed = jnp.stack([inverse_blocks[0], inverse_blocks[1], sigma_end])
    fixed = ordered(fixed, other_core(fixed), 2)
    strips = lax.dynamic_slice_in_dim(fixed, core * STRIP, STRIP, 1)
    base, last_strip, sigma_strip = (strips[0], strips[1], strips[2])
    started = jnp.where(final_group, sigma_strip, jnp.zeros_like(sigma_strip))

    mine = to_chips(copied(factor_blocks, chips))
    inverse_last = inverse_blocks[1:]
    inverse_line = lined(inverse_last, around(inverse_last, 1), 1)
    (mine, mine_first, mine_last, inverse_line, base, last_strip, sigma_strip, started) = (
        lax.optimization_barrier(
            (
                mine,
                mine[:, :1],
                mine[:, 1:],
                inverse_line,
                base,
                last_strip,
                sigma_strip,
                started,
            )
        )
    )
    next_last = hop(mine_last, 1, (2, 4))
    theirs = other_core(mine)
    own = staged([(mine, 0), (mine, 1)], [(theirs, 0), (theirs, 1)])

    strip = (STRIP, nodes)
    state_shape = jax.ShapeDtypeStruct(strip, wide)
    rows_scratch = pltpu.VMEM(strip, wide)

    def packed_shape(count):
        return jax.ShapeDtypeStruct((devices, count * PACK, 128), wide)

    packed = call(first_out, packed_shape(2), [], [last_strip, started], [own])
    first_state = call(
        first_in, state_shape, [rows_scratch] * 2, [to_devices(packed), base], [own]
    )

    def step(base, arrived, factors):
        packed = call(step_out, packed_shape(1), [], [arrived], factors)
        return call(
            step_in, state_shape, [rows_scratch], [to_devices(packed), base], factors
        )

    near, mine_first, next_last = lax.optimization_barrier(
        (hop(first_state, 1, (2, 4, 7)), mine_first, next_last)
    )
    next_first = hop(mine_first, 1, (2, 4))
    state = step(first_state, near, [own])
    state = step(state, hop(state, 1, (6,)), [own])

    pair_state, next_first, next_last, beside = lax.optimization_barrier(
        (state, next_first, next_last, around(inverse_line, SIDE))
    )
    far = hop(pair_state, 2, (5,))
    inverse_mine = lined(inverse_line, beside, SIDE)
    following = staged(
        [(outside(next_first), 0), (outside(next_last), 0)],
        [(outside(other_core(next_first)), 0), (outside(other_core(next_last)), 0)],
    )
    factors = [following, own]
    state = step(pair_state, far, factors)
    far, inverse_theirs = lax.optimization_barrier(
        (hop(state, 2, (3, 5)), other_core(inverse_mine))
    )
    packed = call(last_out, packed_shape(2), [], [far], factors)
    strip_narrow = jax.ShapeDtypeStruct(strip, narrow)
    kept, before = call(
        last_in,
        [strip_narrow, strip_narrow],
        [rows_scratch] * 2,
        [to_devices(packed), near, pair_state, sigma_strip],
        factors,
    )
    copies = call(
        chosen,
        jax.ShapeDtypeStruct((chips,) + strip, narrow),
        [],
        [kept, hop(before, 1, (1, 3, 5, 6, 7))],
        [],
    )
    separator = to_chips(copies)
    block = jax.ShapeDtypeStruct((days, rows, half), narrow)
    square = pltpu.VMEM((nodes, nodes), narrow)
    return pl.pallas_call(
        inner_days,
        out_shape=(block, block),
        in_specs=[vmem] * 6,
        out_specs=(vmem, vmem),
        scratch_shapes=[pltpu.VMEM((nodes // 2, nodes), narrow), square, square]
        + [pltpu.VMEM((nodes, half), narrow)],
        compiler_params=params(),
    )(
        call(own_rows, jax.ShapeDtypeStruct((nodes // 2, nodes), narrow), [], [separator], [own]),
        other_core(separator),
        pinned(own),
        inverse_mine,
        inverse_theirs,
        inverse_blocks[0],
    )


def solution(mesh):
    placed = (P("days", "col", "row"), P("days", "col", "row"), P("col", "row"))
    return jax.shard_map(
        shards,
        mesh=mesh,
        in_specs=placed,
        out_specs=(P("days", "col", "row"), P("days", "col", "row")),
        check_vma=False,
    )
```
